32 devices in a mesh: box: 8 (over z, y), col: 4 (over x, core).
Axes of the slice: x: 2, y: 2, z: 4, core: 2. Of those that a mesh axis runs over, the one named last changes fastest.
Arguments:
- basis: float32 [4, 2, 64, 4096], P(None, None, 'col', 'box'), may hold values from -1000 to 1000
- offsets: float32 [3, 4096], P(None, 'box'), may hold values from -0.5 to 0.5
- weights: float32 [4096], P('box'), may hold values from 0.03 to 0.3
- interp: float32 [32, 32, 128], P('box'), may hold values from 0 to 1
- skeleton: int32 [32, 32], P('box'), may hold values from 0 to 127, as said below
- near_boxes: int32 [32, 27], P('box'), may hold values from 0 to 31, as said below
- near_count: int32 [32], P('box'), may hold values from 3 to 27, as said below
Outputs:
- new_block: float32 [2, 64, 4096], P(None, 'col', 'box')
- coupling: float32 [4, 64, 64], replicated
- factor: float32 [64, 64], replicated
The draws below stay inside these ranges and needn't reach their ends.
Inputs may be any that keep to these rules, and one draw needn't show every extreme that they name: `skeleton`: each row holds 32 different points of the box. `near_boxes`: entry 0 of box b's row is b itself, entry 1 is b + 4 and entry 2 is b - 4, both clipped to the boxes; every entry lies within 4 boxes of b. Box b's near field is the first near_count[b] entries of its row of near_boxes.
All inputs are finite; a program needn't handle non-finite values.
Results may differ from the reference program's by a relative error of at most 0.0003.
Values sent between devices are 32-bit elements; how exact they have to be, the bound alone decides.
A program may use at most 64 MiB of HBM per device.

```python
import math
import jax
import jax.numpy as jnp
from jax import lax

BOX_DEV = 4
P_SIZE = 128
K = 32
NEAR = 27
NC = 64
NPREV = 4
NB = 32
N = 4096


def draw_basis(key, part):
    key_list = jax.random.split(jax.random.fold_in(key, 101), 4)
    shared = jax.random.normal(key_list[0], (1, 2, NC, N), jnp.float32)
    private = jax.random.normal(key_list[1], (NPREV, 2, NC, N), jnp.float32)
    position = 1.0 - (jnp.arange(N, dtype=jnp.int32) // P_SIZE).astype(jnp.float32) / max(NB - 1, 1)
    row_scale = 1.0 + 2.0 * position
    column_scale = 10.0 ** (0.5 * jax.random.uniform(key_list[3], (1, 1, NC, 1), jnp.float32))
    mixing = 0.6
    level = 1.0
    values = (mixing * shared + math.sqrt(1.0 - mixing * mixing) * private + level) * row_scale * column_scale
    return values.astype(jnp.float32)


def draw_skeleton(key, part):
    key_list = jax.random.split(jax.random.fold_in(key, 202), NB)
    orders = jax.vmap(lambda one_key: jax.random.permutation(one_key, P_SIZE))(key_list)
    return orders[:, :K].astype(jnp.int32)


def draw_near_boxes(key, part):
    own_box = jnp.arange(NB, dtype=jnp.int32)[:, None]
    offset = jax.random.randint(jax.random.fold_in(key, 303), (NB, NEAR), -BOX_DEV, BOX_DEV + 1, dtype=jnp.int32)
    slot_index = jnp.arange(NEAR, dtype=jnp.int32)[None, :]
    offset = jnp.where(slot_index == 0, 0, offset)
    offset = jnp.where(slot_index == 1, BOX_DEV, offset)
    offset = jnp.where(slot_index == 2, -BOX_DEV, offset)
    return jnp.clip(own_box + offset, 0, NB - 1).astype(jnp.int32)


def draw_near_count(key, part):
    spread_levels = NEAR - 3
    draw_level = jax.random.randint(jax.random.fold_in(key, 404), (NB,), 0, spread_levels + 1, dtype=jnp.int32)
    near_total = 3 + draw_level * draw_level * draw_level // max(spread_levels * spread_levels, 1)
    return jnp.where(jnp.arange(NB, dtype=jnp.int32) == 0, NEAR, near_total).astype(jnp.int32)


def steps_of(own_key, extent, shards, low, high):
    def one(dim, parts):
        heights = jax.random.uniform(jax.random.fold_in(jax.random.fold_in(own_key, 6), dim), (parts,), jnp.float32, low / len(shards), high / len(shards))
        return jnp.repeat(jnp.exp(heights), extent[dim] // parts).reshape((-1,) + (1,) * (len(extent) - dim - 1))

    factor_of = one(*shards[0])
    for cut in shards[1:]:
        factor_of = factor_of * one(*cut)
    return factor_of


def setup_inputs(seed: int = 0) -> dict:
    streams_of = jax.random.split(jax.random.key(seed), 8)
    return {
        "basis": draw_basis(jax.random.fold_in(streams_of[7], 71), 0),
        "offsets": jnp.clip(jax.random.uniform(streams_of[1], (3, N), jnp.float32, -0.5, 0.5) * steps_of(streams_of[1], (3, N), ((1, 8),), -0.4, 0.0), -0.5, 0.5),
        "weights": jnp.clip(jnp.exp(math.log(0.3) - 2.3025852 * jax.random.uniform(streams_of[2], (N,), jnp.float32) ** steps_of(streams_of[2], (N,), ((0, 8),), -0.2, 0.2)), 0.03, 0.3),
        "interp": jnp.clip(1.0 * jax.random.uniform(streams_of[3], (NB, K, P_SIZE), jnp.float32) ** steps_of(streams_of[3], (NB, K, P_SIZE), ((0, 8),), -0.2, 0.2), 0.0, 1.0),
        "skeleton": draw_skeleton(jax.random.fold_in(streams_of[7], 71), 0),
        "near_boxes": draw_near_boxes(jax.random.fold_in(streams_of[7], 71), 0),
        "near_count": draw_near_count(jax.random.fold_in(streams_of[7], 71), 0),
    }


WAVENUMBER = 6.0
SMOOTHING = 0.1
SHIFT_SCALE = 0.02
EPSILON = 1e-06
HIGHEST = lax.Precision.HIGHEST

def box_centers(box_index):
    along_band = (box_index // BOX_DEV).astype(jnp.float32)
    across = (box_index % BOX_DEV).astype(jnp.float32)
    return jnp.stack([along_band, across, jnp.zeros_like(along_band)])

def helmholtz_pair(targets, sources):
    spread = SMOOTHING * SMOOTHING
    for axis_index in range(3):
        spread = spread + (targets[axis_index][..., :, None] - sources[axis_index][..., None, :]) ** 2
    distance = jnp.sqrt(spread)
    factor = 1.0 / (4.0 * math.pi * distance)
    return (jnp.cos(WAVENUMBER * distance) * factor, jnp.sin(WAVENUMBER * distance) * factor)

def apply_pair(kernel_re, kernel_im, values):
    real_part = jnp.einsum('tq,cq->ct', kernel_re, values[0], precision=HIGHEST) - jnp.einsum('tq,cq->ct', kernel_im, values[1], precision=HIGHEST)
    imag_part = jnp.einsum('tq,cq->ct', kernel_im, values[0], precision=HIGHEST) + jnp.einsum('tq,cq->ct', kernel_re, values[1], precision=HIGHEST)
    return jnp.stack([real_part, imag_part])

def reference(basis, offsets, weights, interp, skeleton, near_boxes, near_count):
    box_index = jnp.arange(NB, dtype=jnp.int32)
    positions = offsets.reshape(3, NB, P_SIZE) + box_centers(box_index)[:, :, None]
    current = basis[NPREV - 1]
    sources = (current * weights).reshape(2, NC, NB, P_SIZE)
    slot_range = jnp.arange(NEAR, dtype=jnp.int32)

    def near_box(box_id):
        listed = near_boxes[box_id]
        live_slot = (slot_range < near_count[box_id]).astype(jnp.float32)
        source_pos = positions[:, listed, :].reshape(3, NEAR * P_SIZE)
        source_val = (sources[:, :, listed, :] * live_slot[None, None, :, None]).reshape(2, NC, NEAR * P_SIZE)
        kernel_re, kernel_im = helmholtz_pair(positions[:, box_id, :], source_pos)
        return apply_pair(kernel_re, kernel_im, source_val)
    near_field = lax.map(near_box, box_index)
    charges = jnp.einsum('bkq,pcbq->pcbk', interp, sources, precision=HIGHEST).reshape(2, NC, NB * K)
    skel_grid = jnp.take_along_axis(positions, jnp.broadcast_to(skeleton[None], (3, NB, K)), axis=2)
    skel_flat = skel_grid.reshape(3, NB * K)

    def far_box(box_id):
        live_slot = slot_range < near_count[box_id]
        listed = jnp.any((near_boxes[box_id][:, None] == box_index[None, :]) & live_slot[:, None], axis=0)
        far_weight = jnp.repeat(1.0 - listed.astype(jnp.float32), K)
        kernel_re, kernel_im = helmholtz_pair(skel_grid[:, box_id, :], skel_flat)
        return apply_pair(kernel_re * far_weight[None, :], kernel_im * far_weight[None, :], charges)
    potentials = lax.map(far_box, box_index)
    far_field = jnp.einsum('bkq,bpck->bpcq', interp, potentials, precision=HIGHEST)
    applied = 0.5 * current + (near_field + far_field).transpose(1, 2, 0, 3).reshape(2, NC, N)
    coupling = jnp.einsum('kpiq,pjq->kij', basis, applied, precision=HIGHEST) / N
    residual = applied - jnp.einsum('kpiq,kij->pjq', basis, coupling, precision=HIGHEST)
    gram_matrix = jnp.einsum('piq,pjq->ij', residual, residual, precision=HIGHEST) / N
    shift_term = SHIFT_SCALE * jnp.trace(gram_matrix) / NC + EPSILON
    lower_factor = jnp.linalg.cholesky(gram_matrix + shift_term * jnp.eye(NC, dtype=jnp.float32))
    flat_rows = residual.transpose(1, 0, 2).reshape(NC, 2 * N)
    solved = jax.scipy.linalg.solve_triangular(lower_factor, flat_rows, lower=True)
    new_block = solved.reshape(NC, 2, N).transpose(1, 0, 2)
    return (new_block, coupling, lower_factor.T)
```

```python
import math

import jax
import jax.numpy as jnp
from jax import lax
from jax.sharding import PartitionSpec as P

BOX_DEV = 4


WAVENUMBER = 6.0
SMOOTHING = 0.1
SHIFT_SCALE = 0.02
EPSILON = 1e-06
HIGHEST = lax.Precision.HIGHEST
SOURCE_BLOCK = 2048


def extended_2(cells, sides, width):
    for axis, dim in sides:
        count = lax.axis_size(axis)
        ends = count - 1
        head = lax.slice_in_dim(cells, 0, width, axis=dim)
        tail = lax.slice_in_dim(cells, cells.shape[dim] - width, cells.shape[dim], axis=dim)
        cells = jnp.concatenate(
            [
                lax.ppermute(tail, axis, [(i, (i + 1) % count) for i in range(ends)]),
                cells,
                lax.ppermute(head, axis, [((i + 1) % count, i) for i in range(ends)]),
            ],
            axis=dim,
        )
    return cells


def box_centers(box_index):
    along_band = (box_index // BOX_DEV).astype(jnp.float32)
    across = (box_index % BOX_DEV).astype(jnp.float32)
    return jnp.stack([along_band, across, jnp.zeros_like(along_band)])


def helmholtz_pair(targets, sources):
    spread = SMOOTHING * SMOOTHING
    for axis_index in range(3):
        spread = (
            spread + (targets[axis_index][..., :, None] - sources[axis_index][..., None, :]) ** 2
        )
    distance = jnp.sqrt(spread)
    factor = 1.0 / (4.0 * math.pi * distance)
    return (jnp.cos(WAVENUMBER * distance) * factor, jnp.sin(WAVENUMBER * distance) * factor)


def far_block(skel_count, target_pos, target_weight, running, shard_piece, first_row):
    value_rows = shard_piece.shape[0] - 3
    source_count = shard_piece.shape[1]
    source_boxes = source_count // skel_count
    target_count = target_pos.shape[1]
    box_weight = lax.dynamic_slice_in_dim(target_weight, first_row // skel_count, source_boxes, 1)
    kernel_re, kernel_im = helmholtz_pair(target_pos, shard_piece[value_rows:])
    kernel_re = (
        kernel_re.reshape(target_count, source_boxes, skel_count) * box_weight[:, :, None]
    ).reshape(target_count, source_count)
    kernel_im = (
        kernel_im.reshape(target_count, source_boxes, skel_count) * box_weight[:, :, None]
    ).reshape(target_count, source_count)
    stacked = jnp.stack([kernel_re, kernel_im])
    charge_rows = shard_piece[:value_rows].reshape(2, value_rows // 2, source_count)
    product = jnp.einsum("gts,pcs->gpct", stacked, charge_rows, precision=HIGHEST)
    return running + jnp.stack([product[0, 0] - product[1, 1], product[1, 0] + product[0, 1]])


def far_fold(skel_count, target_pos, target_weight, running, shard_piece, first_row):
    source_count = shard_piece.shape[1]
    if source_count > SOURCE_BLOCK and source_count % SOURCE_BLOCK == 0:

        def one_block(block_index, carry):
            offset = block_index * SOURCE_BLOCK
            block_piece = lax.dynamic_slice_in_dim(shard_piece, offset, SOURCE_BLOCK, 1)
            return far_block(
                skel_count, target_pos, target_weight, carry, block_piece, first_row + offset
            )

        return lax.fori_loop(0, source_count // SOURCE_BLOCK, one_block, running)
    return far_block(skel_count, target_pos, target_weight, running, shard_piece, first_row)


def gather_by_exchange(piece, axes, count):
    return lax.all_to_all(
        jnp.broadcast_to(piece[None], (count,) + piece.shape), axes, split_axis=0, concat_axis=0
    )


def sum_by_exchange(partial, axes, count):
    rows = partial.shape[0] // count
    pieces = lax.all_to_all(
        partial.reshape((count, rows) + partial.shape[1:]), axes, split_axis=0, concat_axis=0
    )
    return gather_by_exchange(jnp.sum(pieces, axis=0), axes, count).reshape(partial.shape)


def shards(basis, offsets, weights, interp, skeleton, near_boxes, near_count):
    box_count = near_count.shape[0]
    points = interp.shape[2]
    skel_count = interp.shape[1]
    slot_count = near_boxes.shape[1]
    prior_blocks = basis.shape[0]
    columns = basis.shape[2]
    box_size = lax.axis_size("box")
    total_boxes = box_count * box_size
    devices = box_size * lax.axis_size("col")
    first_box = lax.axis_index("box") * box_count
    own_boxes = first_box + jnp.arange(box_count, dtype=jnp.int32)
    positions = offsets.reshape(3, box_count, points) + box_centers(own_boxes)[:, :, None]
    rows_basis = lax.all_to_all(basis, "col", split_axis=3, concat_axis=2, tiled=True)
    current = basis[prior_blocks - 1]
    sources = (current * weights).reshape(2, columns, box_count, points)
    payload = jnp.concatenate([sources.reshape(2 * columns, box_count, points), positions], axis=0)
    extended = extended_2(payload, (("box", 1),), box_count)
    charges = jnp.einsum("bkq,pcbq->pcbk", interp, sources, precision=HIGHEST).reshape(
        2, columns, box_count * skel_count
    )
    hot = (skeleton[:, :, None] == jnp.arange(points, dtype=jnp.int32)).astype(jnp.float32)
    skel_pos = jnp.einsum("bkq,dbq->dbk", hot, positions, precision=HIGHEST).reshape(
        3, box_count * skel_count
    )
    slot_live = jnp.arange(slot_count, dtype=jnp.int32)[None, :] < near_count[:, None]
    payload_far = jnp.concatenate(
        [charges.reshape(2 * columns, box_count * skel_count), skel_pos], axis=0
    )
    gathered = gather_by_exchange(payload_far, "box", box_size)
    gathered = jnp.moveaxis(gathered, 0, 1).reshape(payload_far.shape[0], -1)
    reach = box_count
    window = 2 * reach + 1
    shift_index = jnp.arange(window, dtype=jnp.int32) - reach
    listed = near_boxes[:, :, None] == (own_boxes[:, None] + shift_index[None, :])[:, None, :]
    times = jnp.sum((listed & slot_live[:, :, None]).astype(jnp.float32), axis=1)
    windows = jnp.stack([extended[:, i : i + window] for i in range(box_count)], axis=1)
    source_pos = windows[2 * columns :].reshape(3, box_count, window * points)
    source_val = (windows[: 2 * columns] * times[None, :, :, None]).reshape(
        2, columns, box_count, window * points
    )
    kernel_re, kernel_im = helmholtz_pair(positions, source_pos)
    stacked = jnp.stack([kernel_re, kernel_im])
    product = jnp.einsum("gbtq,pcbq->gpcbt", stacked, source_val, precision=HIGHEST)
    near_field = jnp.stack([product[0, 0] - product[1, 1], product[1, 0] + product[0, 1]])
    every_box = jnp.arange(total_boxes, dtype=jnp.int32)
    box_listed = jnp.any(
        (near_boxes[:, :, None] == every_box[None, None, :]) & slot_live[:, :, None], axis=1
    )
    target_weight = jnp.repeat(1.0 - box_listed.astype(jnp.float32), skel_count, axis=0)
    zero_phi = jnp.zeros((2, columns, box_count * skel_count), jnp.float32)
    potentials = far_fold(
        skel_count, skel_pos, target_weight, zero_phi, gathered, jnp.int32(0)
    )
    potentials = potentials.reshape(2, columns, box_count, skel_count)
    far_field = jnp.einsum("bkq,pcbk->pcbq", interp, potentials, precision=HIGHEST)
    applied = 0.5 * current + (near_field + far_field).reshape(2, columns, box_count * points)
    rows_applied = lax.all_to_all(applied, "col", split_axis=2, concat_axis=1, tiled=True)
    all_columns = rows_applied.shape[1]
    row_total = rows_applied.shape[2] * devices
    part_coupling = (
        jnp.einsum("kpiq,pjq->kij", rows_basis, rows_applied, precision=HIGHEST) / row_total
    ).reshape(prior_blocks * all_columns, all_columns)

    def total(partial):
        if partial.shape[0] % devices == 0 and devices <= 64:
            return sum_by_exchange(partial, ("box", "col"), devices)
        return lax.psum(partial, ("box", "col"))

    coupling = total(part_coupling).reshape(prior_blocks, all_columns, all_columns)
    residual = rows_applied - jnp.einsum("kpiq,kij->pjq", rows_basis, coupling, precision=HIGHEST)
    gram_matrix = total(
        jnp.einsum("piq,pjq->ij", residual, residual, precision=HIGHEST) / row_total
    )
    identity = jnp.eye(all_columns, dtype=jnp.float32)
    shift_term = SHIFT_SCALE * jnp.trace(gram_matrix) / all_columns + EPSILON
    lower_factor = jnp.linalg.cholesky(gram_matrix + shift_term * identity)
    inverse = jax.scipy.linalg.solve_triangular(lower_factor, identity, lower=True)
    normalized = jnp.einsum("ij,pjq->piq", inverse, residual, precision=HIGHEST)
    new_block = lax.all_to_all(normalized, "col", split_axis=1, concat_axis=2, tiled=True)
    return (new_block, coupling, lower_factor.T)


def solution(mesh):
    return jax.shard_map(
        shards,
        mesh=mesh,
        in_specs=(
            P(None, None, "col", "box"),
            P(None, "box"),
            P("box"),
            P("box", None, None),
            P("box", None),
            P("box", None),
            P("box"),
        ),
        out_specs=(P(None, "col", "box"), P(), P()),
        check_vma=False,
    )
```

```python
import functools
import math

import jax
import jax.numpy as jnp
from jax import lax
from jax.experimental import pallas as pl
from jax.experimental.pallas import tpu as pltpu
from jax.sharding import PartitionSpec as P

BOX_DEV = 4


WAVENUMBER = 6.0
SMOOTHING = 0.1
SHIFT_SCALE = 0.02
EPSILON = 1e-06
HIGHEST = lax.Precision.HIGHEST
SOURCE_BLOCK = 2048


def extended_2(cells, sides, width):
    for axis, dim in sides:
        count = lax.axis_size(axis)
        ends = count - 1
        head = lax.slice_in_dim(cells, 0, width, axis=dim)
        tail = lax.slice_in_dim(cells, cells.shape[dim] - width, cells.shape[dim], axis=dim)
        cells = jnp.concatenate(
            [
                lax.ppermute(tail, axis, [(i, (i + 1) % count) for i in range(ends)]),
                cells,
                lax.ppermute(head, axis, [((i + 1) % count, i) for i in range(ends)]),
            ],
            axis=dim,
        )
    return cells


def box_centers(box_index):
    along_band = (box_index // BOX_DEV).astype(jnp.float32)
    across = (box_index % BOX_DEV).astype(jnp.float32)
    return jnp.stack([along_band, across, jnp.zeros_like(along_band)])


def helmholtz_pair(targets, sources):
    spread = SMOOTHING * SMOOTHING
    for axis_index in range(3):
        spread = (
            spread + (targets[axis_index][..., :, None] - sources[axis_index][..., None, :]) ** 2
        )
    distance = jnp.sqrt(spread)
    factor = 1.0 / (4.0 * math.pi * distance)
    return (jnp.cos(WAVENUMBER * distance) * factor, jnp.sin(WAVENUMBER * distance) * factor)


def far_block(skel_count, target_pos, target_weight, running, shard_piece, first_row):
    value_rows = shard_piece.shape[0] - 3
    source_count = shard_piece.shape[1]
    source_boxes = source_count // skel_count
    target_count = target_pos.shape[1]
    box_weight = lax.dynamic_slice_in_dim(target_weight, first_row // skel_count, source_boxes, 1)
    kernel_re, kernel_im = helmholtz_pair(target_pos, shard_piece[value_rows:])
    kernel_re = (
        kernel_re.reshape(target_count, source_boxes, skel_count) * box_weight[:, :, None]
    ).reshape(target_count, source_count)
    kernel_im = (
        kernel_im.reshape(target_count, source_boxes, skel_count) * box_weight[:, :, None]
    ).reshape(target_count, source_count)
    stacked = jnp.stack([kernel_re, kernel_im])
    charge_rows = shard_piece[:value_rows].reshape(2, value_rows // 2, source_count)
    product = jnp.einsum("gts,pcs->gpct", stacked, charge_rows, precision=HIGHEST)
    return running + jnp.stack([product[0, 0] - product[1, 1], product[1, 0] + product[0, 1]])


def far_fold(skel_count, target_pos, target_weight, running, shard_piece, first_row):
    source_count = shard_piece.shape[1]
    if source_count > SOURCE_BLOCK and source_count % SOURCE_BLOCK == 0:

        def one_block(block_index, carry):
            offset = block_index * SOURCE_BLOCK
            block_piece = lax.dynamic_slice_in_dim(shard_piece, offset, SOURCE_BLOCK, 1)
            return far_block(
                skel_count, target_pos, target_weight, carry, block_piece, first_row + offset
            )

        return lax.fori_loop(0, source_count // SOURCE_BLOCK, one_block, running)
    return far_block(skel_count, target_pos, target_weight, running, shard_piece, first_row)


def gather_by_exchange(piece, axes, count):
    return lax.all_to_all(
        jnp.broadcast_to(piece[None], (count,) + piece.shape), axes, split_axis=0, concat_axis=0
    )


def peer_copy(axis, count, step, source, target, sems):
    peer = lax.rem(lax.axis_index(axis) + step, count)
    return pltpu.make_async_remote_copy(
        src_ref=source(peer),
        dst_ref=target,
        send_sem=sems[0].at[step],
        recv_sem=sems[1].at[step],
        device_id={axis: peer},
        device_id_type=pl.DeviceIdType.MESH,
    )


def start_all(axis, count, source, target, sems):
    def body(step, carry):
        peer_copy(axis, count, step, source, target, sems).start()
        return carry

    lax.fori_loop(1, count, body, 0)


def wait_all(axis, count, source, target, sems):
    def body(step, carry):
        peer_copy(axis, count, step, source, target, sems).wait()
        return carry

    lax.fori_loop(1, count, body, 0)


def exchange(axis, count, source, target, sems):
    start_all(axis, count, source, target, sems)
    wait_all(axis, count, source, target, sems)


def slot_sum(buffer, count):
    if count <= 16:
        total = buffer[0]
        for slot in range(1, count):
            total = total + buffer[slot]
        return total
    return lax.fori_loop(1, count, lambda slot, total: total + buffer[slot], buffer[0])


def greet(box_size, col_size):
    barrier = pltpu.get_barrier_semaphore()
    for axis, count in (("box", box_size), ("col", col_size)):

        def body(step, carry):
            peer = lax.rem(lax.axis_index(axis) + step, count)
            pl.semaphore_signal(
                barrier, inc=1, device_id={axis: peer}, device_id_type=pl.DeviceIdType.MESH
            )
            return carry

        lax.fori_loop(1, count, body, 0)
    pl.semaphore_wait(barrier, box_size + col_size - 2)


def nt_dot(left, right):
    return lax.dot_general(
        left,
        right,
        (((1,), (1,)), ((), ())),
        precision=HIGHEST,
        preferred_element_type=jnp.float32,
    )


def nn_dot(left, right):
    return jnp.dot(left, right, precision=HIGHEST, preferred_element_type=jnp.float32)


def factor_rows(matrix, size):
    row_index = lax.broadcasted_iota(jnp.int32, matrix.shape, 0)
    scale = jnp.zeros((size, 1), jnp.float32)
    row_column = lax.broadcasted_iota(jnp.int32, (size, 1), 0)
    for step in range(size):
        pivot = matrix[step : step + 1, step : step + 1]
        row = matrix[step : step + 1, :] * (1.0 / pivot)
        column = matrix[:, step : step + 1]
        scale = jnp.where(row_column == step, pivot, scale)
        matrix = matrix - jnp.where(row_index > step, column * row, 0.0)
    return matrix * lax.rsqrt(scale)


def tail_kernel(
    box_size,
    col_size,
    basis_ref,
    applied_ref,
    block_ref,
    coupling_ref,
    factor_ref,
    row_basis,
    row_applied,
    part,
    col_parts,
    box_parts,
    piece,
    whole,
    gram_mine,
    gram_cols,
    gram_sum,
    gram_boxes,
    normal,
    *sems,
):
    sems = [(sems[2 * i], sems[2 * i + 1]) for i in range(8)]
    prior, _, columns, _ = basis_ref.shape
    all_columns, points = row_applied.shape[1:]
    col = lax.axis_index("col")
    box = lax.axis_index("box")
    share = all_columns // col_size
    row_total = points * box_size * col_size

    def rows_of(index, size):
        return pl.ds(pl.multiple_of(index * size, size), size)

    def basis_source(peer):
        return basis_ref.at[:, :, :, rows_of(peer, points)]

    def applied_source(peer):
        return applied_ref.at[:, :, rows_of(peer, points)]

    basis_target = row_basis.at[:, :, rows_of(col, columns), :]
    applied_target = row_applied.at[:, rows_of(col, columns), :]
    greet(box_size, col_size)
    start_all("col", col_size, applied_source, applied_target, sems[1])
    start_all("col", col_size, basis_source, basis_target, sems[0])
    row_basis[:, :, rows_of(col, columns), :] = basis_ref[:, :, :, rows_of(col, points)]
    row_applied[:, rows_of(col, columns), :] = applied_ref[:, :, rows_of(col, points)]
    wait_all("col", col_size, applied_source, applied_target, sems[1])
    wait_all("col", col_size, basis_source, basis_target, sems[0])
    flat_basis = jnp.concatenate(
        [
            row_basis[:, part_index].reshape(prior * all_columns, points)
            for part_index in range(2)
        ],
        axis=1,
    )
    flat_applied = jnp.concatenate([row_applied[0], row_applied[1]], axis=1)
    part[...] = nt_dot(flat_applied, flat_basis) * (1.0 / row_total)
    col_parts[col] = part[rows_of(col, share), :]
    exchange(
        "col", col_size, lambda peer: part.at[rows_of(peer, share), :], col_parts.at[col], sems[2]
    )
    piece[...] = slot_sum(col_parts, col_size)
    box_parts[box] = piece[...]
    exchange("box", box_size, lambda peer: piece, box_parts.at[box], sems[3])
    shared = slot_sum(box_parts, box_size)
    whole[rows_of(col, share), :] = shared
    piece[...] = shared
    exchange("col", col_size, lambda peer: piece, whole.at[rows_of(col, share), :], sems[4])
    coupling = whole[...]
    residual = flat_applied - nn_dot(coupling, flat_basis)
    blank = jnp.zeros_like(residual)
    gram_mine[...] = nt_dot(residual, jnp.concatenate([residual, blank], axis=0)) * (
        1.0 / row_total
    )
    gram_cols[col] = gram_mine[...]
    gram_source = lambda peer: gram_mine
    start_all("col", col_size, gram_source, gram_cols.at[col], sems[5])
    coupling_ref[...] = coupling.T
    wait_all("col", col_size, gram_source, gram_cols.at[col], sems[5])
    gram_sum[...] = slot_sum(gram_cols, col_size)
    gram_boxes[box] = gram_sum[...]
    exchange("box", box_size, lambda peer: gram_sum, gram_boxes.at[box], sems[6])
    gram = slot_sum(gram_boxes, box_size)
    row_index = lax.broadcasted_iota(jnp.int32, gram.shape, 0)
    lane_index = lax.broadcasted_iota(jnp.int32, gram.shape, 1)
    trace = jnp.sum(jnp.where(row_index == lane_index, gram, 0.0), keepdims=True)
    shift = trace * (SHIFT_SCALE / all_columns) + EPSILON
    matrix = gram + jnp.where(row_index == lane_index, shift, 0.0)
    matrix = matrix + jnp.where(row_index + all_columns == lane_index, 1.0, 0.0)
    reduced = factor_rows(matrix, all_columns)
    factor_ref[...] = jnp.where(lane_index >= row_index, reduced, 0.0)
    inverse = jnp.where(lane_index >= all_columns, reduced, 0.0)
    normalized = nn_dot(inverse, jnp.concatenate([blank, residual], axis=0))
    normal[0] = normalized[:, :points]
    normal[1] = normalized[:, points:]
    block_ref[:, :, rows_of(col, points)] = normal[:, rows_of(col, columns), :]
    exchange(
        "col",
        col_size,
        lambda peer: normal.at[:, rows_of(peer, columns), :],
        block_ref.at[:, :, rows_of(col, points)],
        sems[7],
    )


def tail(basis, applied):
    prior, parts, columns, local_points = basis.shape
    box_size, col_size = lax.axis_size("box"), lax.axis_size("col")
    all_columns, points = columns * col_size, local_points // col_size
    share = all_columns // col_size
    flat = prior * all_columns
    square = (all_columns, 2 * all_columns)
    shapes = [
        (prior, parts, all_columns, points),
        (parts, all_columns, points),
        (all_columns, flat),
        (col_size, share, flat),
        (box_size, share, flat),
        (share, flat),
        (all_columns, flat),
        square,
        (col_size,) + square,
        square,
        (box_size,) + square,
        (parts, all_columns, points),
    ]
    sems = []
    for axis in ("col", "col", "col", "box", "col", "col", "box", "col"):
        count = box_size if axis == "box" else col_size
        sems += [pltpu.SemaphoreType.DMA((count,))] * 2
    vmem = pl.BlockSpec(memory_space=pltpu.VMEM)
    block, coupling, factor = pl.pallas_call(
        functools.partial(tail_kernel, box_size, col_size),
        out_shape=(
            jax.ShapeDtypeStruct((parts, columns, local_points), jnp.float32),
            jax.ShapeDtypeStruct((flat, all_columns), jnp.float32),
            jax.ShapeDtypeStruct(square, jnp.float32),
        ),
        in_specs=[vmem] * 2,
        out_specs=(vmem,) * 3,
        scratch_shapes=[pltpu.VMEM(shape, jnp.float32) for shape in shapes] + sems,
        compiler_params=pltpu.CompilerParams(
            collective_id=0, has_side_effects=True, vmem_limit_bytes=40 * 1024 * 1024
        ),
    )(basis, applied)
    coupling = coupling.reshape(prior, all_columns, all_columns)
    return block, coupling, factor[:, :all_columns]


def shards(basis, offsets, weights, interp, skeleton, near_boxes, near_count):
    box_count = near_count.shape[0]
    points = interp.shape[2]
    skel_count = interp.shape[1]
    slot_count = near_boxes.shape[1]
    prior_blocks = basis.shape[0]
    columns = basis.shape[2]
    box_size = lax.axis_size("box")
    total_boxes = box_count * box_size
    first_box = lax.axis_index("box") * box_count
    own_boxes = first_box + jnp.arange(box_count, dtype=jnp.int32)
    positions = offsets.reshape(3, box_count, points) + box_centers(own_boxes)[:, :, None]
    current = basis[prior_blocks - 1]
    sources = (current * weights).reshape(2, columns, box_count, points)
    payload = jnp.concatenate([sources.reshape(2 * columns, box_count, points), positions], axis=0)
    extended = extended_2(payload, (("box", 1),), box_count)
    charges = jnp.einsum("bkq,pcbq->pcbk", interp, sources, precision=HIGHEST).reshape(
        2, columns, box_count * skel_count
    )
    hot = (skeleton[:, :, None] == jnp.arange(points, dtype=jnp.int32)).astype(jnp.float32)
    skel_pos = jnp.einsum("bkq,dbq->dbk", hot, positions, precision=HIGHEST).reshape(
        3, box_count * skel_count
    )
    slot_live = jnp.arange(slot_count, dtype=jnp.int32)[None, :] < near_count[:, None]
    payload_far = jnp.concatenate(
        [charges.reshape(2 * columns, box_count * skel_count), skel_pos], axis=0
    )
    gathered = gather_by_exchange(payload_far, "box", box_size)
    gathered = jnp.moveaxis(gathered, 0, 1).reshape(payload_far.shape[0], -1)
    reach = box_count
    window = 2 * reach + 1
    shift_index = jnp.arange(window, dtype=jnp.int32) - reach
    listed = near_boxes[:, :, None] == (own_boxes[:, None] + shift_index[None, :])[:, None, :]
    times = jnp.sum((listed & slot_live[:, :, None]).astype(jnp.float32), axis=1)
    windows = jnp.stack([extended[:, i : i + window] for i in range(box_count)], axis=1)
    source_pos = windows[2 * columns :].reshape(3, box_count, window * points)
    source_val = (windows[: 2 * columns] * times[None, :, :, None]).reshape(
        2, columns, box_count, window * points
    )
    kernel_re, kernel_im = helmholtz_pair(positions, source_pos)
    stacked = jnp.stack([kernel_re, kernel_im])
    product = jnp.einsum("gbtq,pcbq->gpcbt", stacked, source_val, precision=HIGHEST)
    near_field = jnp.stack([product[0, 0] - product[1, 1], product[1, 0] + product[0, 1]])
    every_box = jnp.arange(total_boxes, dtype=jnp.int32)
    box_listed = jnp.any(
        (near_boxes[:, :, None] == every_box[None, None, :]) & slot_live[:, :, None], axis=1
    )
    target_weight = jnp.repeat(1.0 - box_listed.astype(jnp.float32), skel_count, axis=0)
    zero_phi = jnp.zeros((2, columns, box_count * skel_count), jnp.float32)
    potentials = far_fold(
        skel_count, skel_pos, target_weight, zero_phi, gathered, jnp.int32(0)
    )
    potentials = potentials.reshape(2, columns, box_count, skel_count)
    far_field = jnp.einsum("bkq,pcbk->pcbq", interp, potentials, precision=HIGHEST)
    applied = 0.5 * current + (near_field + far_field).reshape(2, columns, box_count * points)
    return tail(basis, applied)


def solution(mesh):
    return jax.shard_map(
        shards,
        mesh=mesh,
        in_specs=(
            P(None, None, "col", "box"),
            P(None, "box"),
            P("box"),
            P("box", None, None),
            P("box", None),
            P("box", None),
            P("box"),
        ),
        out_specs=(P(None, "col", "box"), P(), P()),
        check_vma=False,
    )
```

```python
import functools
import math

import jax
import jax.numpy as jnp
from jax import lax
from jax.experimental import pallas as pl
from jax.experimental.pallas import tpu as pltpu
from jax.sharding import PartitionSpec as P

BOX_DEV = 4


WAVENUMBER = 6.0
SMOOTHING = 0.1
SHIFT_SCALE = 0.02
EPSILON = 1e-06
HIGHEST = lax.Precision.HIGHEST


def split(values):
    high = values.astype(jnp.bfloat16)
    return high, (values - high.astype(jnp.float32)).astype(jnp.bfloat16)


def pair_dot(values, kernel):
    rows = values.shape[0]
    value_high, value_low = split(values)
    kernel_high, kernel_low = split(kernel)
    both = jnp.dot(
        jnp.concatenate([value_high, value_low], axis=0),
        kernel_high,
        preferred_element_type=jnp.float32,
    )
    cross = jnp.dot(value_high, kernel_low, preferred_element_type=jnp.float32)
    return both[:rows] + both[rows:] + cross


def helmholtz_pair(sources, targets):
    spread = SMOOTHING * SMOOTHING
    for axis_index in range(3):
        step = sources[:, axis_index : axis_index + 1] - targets[axis_index : axis_index + 1, :]
        spread = spread + step * step
    inverse = lax.rsqrt(spread)
    angle = WAVENUMBER * (spread * inverse)
    factor = inverse * (1.0 / (4.0 * math.pi))
    turns = jnp.floor(angle * (2.0 / math.pi) + 0.5)
    quarter = turns.astype(jnp.int32)
    rest = angle - turns * 1.5703125
    rest = rest - turns * 4.837512969970703125e-4
    rest = rest - turns * 7.54978995489188216e-8
    square = rest * rest
    sine = (-1.9515295891e-4 * square + 8.3321608736e-3) * square - 1.6666654611e-1
    sine = sine * square * rest + rest
    cosine = (2.443315711809948e-5 * square - 1.388731625493765e-3) * square
    cosine = (cosine + 4.166664568298827e-2) * square * square - 0.5 * square + 1.0
    odd = (quarter & 1) == 1
    sine, cosine = jnp.where(odd, cosine, sine), jnp.where(odd, sine, cosine)
    sine_factor = jnp.where((quarter & 2) == 2, -factor, factor)
    cosine_factor = jnp.where(((quarter + 1) & 2) == 2, -factor, factor)
    return cosine * cosine_factor, sine * sine_factor


def combine(product, columns, points):
    left, right = product[:, :points], product[:, points:]
    return jnp.concatenate(
        [left[:columns] - right[columns:], left[columns:] + right[:columns]], axis=0
    )


def peer_copy(axis, count, step, source, target, sems):
    peer = lax.rem(lax.axis_index(axis) + step, count)
    return pltpu.make_async_remote_copy(
        src_ref=source(peer),
        dst_ref=target,
        send_sem=sems[0].at[step],
        recv_sem=sems[1].at[step],
        device_id={axis: peer},
        device_id_type=pl.DeviceIdType.MESH,
    )


def start_all(axis, count, source, target, sems):
    def body(step, carry):
        peer_copy(axis, count, step, source, target, sems).start()
        return carry

    lax.fori_loop(1, count, body, 0)


def wait_all(axis, count, source, target, sems):
    def body(step, carry):
        peer_copy(axis, count, step, source, target, sems).wait()
        return carry

    lax.fori_loop(1, count, body, 0)


def exchange(axis, count, source, target, sems):
    start_all(axis, count, source, target, sems)
    wait_all(axis, count, source, target, sems)


def slot_sum(buffer, count):
    if count <= 16:
        total = buffer[0]
        for slot in range(1, count):
            total = total + buffer[slot]
        return total
    return lax.fori_loop(1, count, lambda slot, total: total + buffer[slot], buffer[0])


def greet(barrier, box_size, col_size):
    for axis, count in (("box", box_size), ("col", col_size)):

        def body(step, carry):
            peer = lax.rem(lax.axis_index(axis) + step, count)
            pl.semaphore_signal(
                barrier, inc=1, device_id={axis: peer}, device_id_type=pl.DeviceIdType.MESH
            )
            return carry

        lax.fori_loop(1, count, body, 0)


def nt_dot(left, right):
    return lax.dot_general(
        left,
        right,
        (((1,), (1,)), ((), ())),
        precision=HIGHEST,
        preferred_element_type=jnp.float32,
    )


def nn_dot(left, right):
    return jnp.dot(left, right, precision=HIGHEST, preferred_element_type=jnp.float32)


def factor_rows(matrix, size):
    row_index = lax.broadcasted_iota(jnp.int32, matrix.shape, 0)
    scale = jnp.zeros((size, 1), jnp.float32)
    row_column = lax.broadcasted_iota(jnp.int32, (size, 1), 0)
    for step in range(size):
        pivot = matrix[step : step + 1, step : step + 1]
        row = matrix[step : step + 1, :] * (1.0 / pivot)
        column = matrix[:, step : step + 1]
        scale = jnp.where(row_column == step, pivot, scale)
        matrix = matrix - jnp.where(row_index > step, column * row, 0.0)
    return matrix * lax.rsqrt(scale)


def step_kernel(
    box_size,
    col_size,
    basis_ref,
    offsets_ref,
    weights_ref,
    interp_ref,
    skeleton_ref,
    near_boxes_ref,
    near_count_ref,
    block_ref,
    coupling_ref,
    factor_ref,
    row_basis,
    row_applied,
    part,
    col_parts,
    box_parts,
    piece,
    whole,
    gram_mine,
    gram_cols,
    gram_sum,
    gram_boxes,
    normal,
    applied_ref,
    beside,
    column_pos,
    far_mine,
    far_all,
    near_times,
    far_times,
    near_total,
    far_total,
    *sems,
):
    sems = [(sems[2 * i], sems[2 * i + 1]) for i in range(11)]
    prior, _, columns, _ = basis_ref.shape
    all_columns, points = row_applied.shape[1:]
    col = lax.axis_index("col")
    box = lax.axis_index("box")
    share = all_columns // col_size
    row_total = points * box_size * col_size

    def rows_of(index, size):
        return pl.ds(pl.multiple_of(index * size, size), size)

    def basis_source(peer):
        return basis_ref.at[:, :, :, rows_of(peer, points)]

    def applied_source(peer):
        return applied_ref.at[:, :, rows_of(peer, points)]

    basis_target = row_basis.at[:, :, rows_of(col, columns), :]
    applied_target = row_applied.at[:, rows_of(col, columns), :]
    box_count, skel_count, box_points = interp_ref.shape
    rows = 2 * columns
    reach = box_count
    window = 2 * reach + 1
    first_box = box * box_count
    barrier = pltpu.get_barrier_semaphore()
    greet(barrier, box_size, col_size)

    def of_box(index):
        return slice(index * box_points, (index + 1) * box_points)

    local_points = box_count * box_points
    box_lane = lax.broadcasted_iota(jnp.int32, (1, local_points), 1) // box_points + first_box
    center_first = (box_lane // BOX_DEV).astype(jnp.float32)
    center_second = (box_lane % BOX_DEV).astype(jnp.float32)
    positions = jnp.concatenate(
        [
            offsets_ref[0:1, :] + center_first,
            offsets_ref[1:2, :] + center_second,
            offsets_ref[2:3, :],
            jnp.zeros((5, local_points), jnp.float32),
        ],
        axis=0,
    )
    current = basis_ref[prior - 1].reshape(rows, local_points)
    sources = current * weights_ref[...]
    beside[1, :rows, :] = sources
    beside[1, rows:, :] = positions
    pl.semaphore_wait(barrier, box_size + col_size - 2)
    after = lax.rem(box + 1, box_size)
    before = lax.rem(box + box_size - 1, box_size)
    side_copies = [
        pltpu.make_async_remote_copy(
            src_ref=beside.at[1],
            dst_ref=beside.at[slot],
            send_sem=sems[index][0].at[0],
            recv_sem=sems[index][1].at[0],
            device_id={"box": peer},
            device_id_type=pl.DeviceIdType.MESH,
        )
        for slot, peer, index in ((0, after, 8), (2, before, 9))
    ]
    for copy in side_copies:
        copy.start()
    flat_skel = box_count * skel_count
    interp = interp_ref[...].reshape(flat_skel, box_points)
    skel_box = lax.broadcasted_iota(jnp.int32, (1, flat_skel), 1) // skel_count
    skel_flat = jnp.concatenate([skeleton_ref[b : b + 1, :] for b in range(box_count)], axis=1)
    hot = (
        lax.broadcasted_iota(jnp.int32, (box_points, flat_skel), 0) == skel_flat
    ).astype(jnp.float32)
    charges = jnp.zeros((rows, flat_skel), jnp.float32)
    skel_pos = jnp.zeros((8, flat_skel), jnp.float32)
    stacked = nt_dot(
        jnp.concatenate([sources[:, of_box(b)] for b in range(box_count)], axis=0), interp
    )
    stacked_pos = nn_dot(
        jnp.concatenate([positions[:, of_box(b)] for b in range(box_count)], axis=0), hot
    )
    for b in range(box_count):
        charges = jnp.where(skel_box == b, stacked[b * rows : (b + 1) * rows], charges)
        skel_pos = jnp.where(skel_box == b, stacked_pos[b * 8 : (b + 1) * 8], skel_pos)
    far_mine[:rows, :] = charges
    far_mine[rows:, :] = skel_pos
    far_all[box] = far_mine[...]
    far_source = lambda peer: far_mine
    start_all("box", box_size, far_source, far_all.at[box], sems[10])
    start_all("col", col_size, basis_source, basis_target, sems[0])
    own_box = lax.broadcasted_iota(jnp.int32, (box_count, 1), 0) + first_box
    slots = lax.broadcasted_iota(jnp.int32, near_boxes_ref.shape, 1)
    distance = jnp.where(slots < near_count_ref[...], near_boxes_ref[...] - own_box, window)
    for o in range(window):
        times = jnp.sum((distance == o - reach).astype(jnp.float32), axis=1, keepdims=True)
        near_times[o] = jnp.broadcast_to(times, (box_count, box_points))
        listed = jnp.zeros((1, flat_skel), jnp.float32)
        for b in range(box_count):
            listed = jnp.where(skel_box == b, jnp.minimum(times[b : b + 1], 1.0), listed)
        far_times[o : o + 1, :] = listed
    near_total[...] = jnp.zeros_like(near_total)
    far_total[...] = jnp.zeros_like(far_total)
    for copy in side_copies:
        copy.wait()
    for slot in range(3):
        column_pos[slot * local_points : (slot + 1) * local_points, :] = beside[slot, rows:, :].T

    def near_step(o, carry):
        for b in range(box_count):
            extended = o + b
            lanes = rows_of(lax.rem(extended, box_count), box_points)
            values = beside[extended // box_count, :rows, lanes]
            values = values * near_times[o, b : b + 1, :]
            source_pos = column_pos[rows_of(extended, box_points), :]
            kernel = helmholtz_pair(source_pos, beside[1, rows:, of_box(b)])
            near_total[b] += pair_dot(values, jnp.concatenate(kernel, axis=1))
        return carry

    lax.fori_loop(0, window, near_step, 0)
    wait_all("box", box_size, far_source, far_all.at[box], sems[10])

    def far_step(slot, carry):
        source_pos = far_all[slot, rows:, :].T
        kernel_re, kernel_im = helmholtz_pair(source_pos, far_mine[rows:, :])
        source_box = lax.broadcasted_iota(jnp.int32, kernel_re.shape, 0) // skel_count
        offset = source_box + (slot * box_count - first_box + reach) - skel_box
        weight = jnp.ones_like(kernel_re)
        for o in range(window):
            weight = jnp.where(offset == o, 1.0 - far_times[o : o + 1, :], weight)
        kernel = jnp.concatenate([kernel_re * weight, kernel_im * weight], axis=1)
        far_total[...] += pair_dot(far_all[slot, :rows, :], kernel)
        return carry

    lax.fori_loop(0, box_size, far_step, 0)
    potentials = combine(far_total[...], columns, flat_skel)
    far_field = nn_dot(
        jnp.concatenate(
            [jnp.where(skel_box == b, potentials, 0.0) for b in range(box_count)], axis=0
        ),
        interp,
    )
    for b in range(box_count):
        field = combine(near_total[b], columns, box_points) + far_field[b * rows : (b + 1) * rows]
        field = 0.5 * current[:, of_box(b)] + field
        applied_ref[0, :, of_box(b)] = field[:columns]
        applied_ref[1, :, of_box(b)] = field[columns:]
    start_all("col", col_size, applied_source, applied_target, sems[1])
    row_basis[:, :, rows_of(col, columns), :] = basis_ref[:, :, :, rows_of(col, points)]
    row_applied[:, rows_of(col, columns), :] = applied_ref[:, :, rows_of(col, points)]
    wait_all("col", col_size, applied_source, applied_target, sems[1])
    wait_all("col", col_size, basis_source, basis_target, sems[0])
    flat_basis = jnp.concatenate(
        [
            row_basis[:, part_index].reshape(prior * all_columns, points)
            for part_index in range(2)
        ],
        axis=1,
    )
    flat_applied = jnp.concatenate([row_applied[0], row_applied[1]], axis=1)
    part[...] = nt_dot(flat_applied, flat_basis) * (1.0 / row_total)
    col_parts[col] = part[rows_of(col, share), :]
    exchange(
        "col", col_size, lambda peer: part.at[rows_of(peer, share), :], col_parts.at[col], sems[2]
    )
    piece[...] = slot_sum(col_parts, col_size)
    box_parts[box] = piece[...]
    exchange("box", box_size, lambda peer: piece, box_parts.at[box], sems[3])
    shared = slot_sum(box_parts, box_size)
    whole[rows_of(col, share), :] = shared
    piece[...] = shared
    exchange("col", col_size, lambda peer: piece, whole.at[rows_of(col, share), :], sems[4])
    coupling = whole[...]
    residual = flat_applied - nn_dot(coupling, flat_basis)
    blank = jnp.zeros_like(residual)
    gram_mine[...] = nt_dot(residual, jnp.concatenate([residual, blank], axis=0)) * (
        1.0 / row_total
    )
    gram_cols[col] = gram_mine[...]
    gram_source = lambda peer: gram_mine
    start_all("col", col_size, gram_source, gram_cols.at[col], sems[5])
    coupling_ref[...] = coupling.T
    wait_all("col", col_size, gram_source, gram_cols.at[col], sems[5])
    gram_sum[...] = slot_sum(gram_cols, col_size)
    gram_boxes[box] = gram_sum[...]
    exchange("box", box_size, lambda peer: gram_sum, gram_boxes.at[box], sems[6])
    gram = slot_sum(gram_boxes, box_size)
    row_index = lax.broadcasted_iota(jnp.int32, gram.shape, 0)
    lane_index = lax.broadcasted_iota(jnp.int32, gram.shape, 1)
    trace = jnp.sum(jnp.where(row_index == lane_index, gram, 0.0), keepdims=True)
    shift = trace * (SHIFT_SCALE / all_columns) + EPSILON
    matrix = gram + jnp.where(row_index == lane_index, shift, 0.0)
    matrix = matrix + jnp.where(row_index + all_columns == lane_index, 1.0, 0.0)
    reduced = factor_rows(matrix, all_columns)
    factor_ref[...] = jnp.where(lane_index >= row_index, reduced, 0.0)
    inverse = jnp.where(lane_index >= all_columns, reduced, 0.0)
    normalized = nn_dot(inverse, jnp.concatenate([blank, residual], axis=0))
    normal[0] = normalized[:, :points]
    normal[1] = normalized[:, points:]
    block_ref[:, :, rows_of(col, points)] = normal[:, rows_of(col, columns), :]
    exchange(
        "col",
        col_size,
        lambda peer: normal.at[:, rows_of(peer, columns), :],
        block_ref.at[:, :, rows_of(col, points)],
        sems[7],
    )


def shards(basis, offsets, weights, interp, skeleton, near_boxes, near_count):
    prior, parts, columns, local_points = basis.shape
    box_count, skel_count, box_points = interp.shape
    flat_skel = box_count * skel_count
    rows = parts * columns
    window = 2 * box_count + 1
    box_size, col_size = lax.axis_size("box"), lax.axis_size("col")
    all_columns, points = columns * col_size, local_points // col_size
    share = all_columns // col_size
    flat = prior * all_columns
    square = (all_columns, 2 * all_columns)
    shapes = [
        (prior, parts, all_columns, points),
        (parts, all_columns, points),
        (all_columns, flat),
        (col_size, share, flat),
        (box_size, share, flat),
        (share, flat),
        (all_columns, flat),
        square,
        (col_size,) + square,
        square,
        (box_size,) + square,
        (parts, all_columns, points),
        (parts, columns, local_points),
        (3, rows + 8, local_points),
        (3 * local_points, 8),
        (rows + 8, flat_skel),
        (box_size, rows + 8, flat_skel),
        (window, box_count, box_points),
        (window, flat_skel),
        (box_count, rows, 2 * box_points),
        (rows, 2 * flat_skel),
    ]
    sems = []
    for axis in ("col", "col", "col", "box", "col", "col", "box", "col", "", "", "box"):
        count = {"box": box_size, "col": col_size, "": 1}[axis]
        sems += [pltpu.SemaphoreType.DMA((count,))] * 2
    vmem = pl.BlockSpec(memory_space=pltpu.VMEM)
    block, coupling, factor = pl.pallas_call(
        functools.partial(step_kernel, box_size, col_size),
        out_shape=(
            jax.ShapeDtypeStruct((parts, columns, local_points), jnp.float32),
            jax.ShapeDtypeStruct((flat, all_columns), jnp.float32),
            jax.ShapeDtypeStruct(square, jnp.float32),
        ),
        in_specs=[vmem] * 7,
        out_specs=(vmem,) * 3,
        scratch_shapes=[pltpu.VMEM(shape, jnp.float32) for shape in shapes] + sems,
        compiler_params=pltpu.CompilerParams(
            collective_id=0, has_side_effects=True, vmem_limit_bytes=40 * 1024 * 1024
        ),
    )(
        basis,
        offsets,
        weights.reshape(1, local_points),
        interp,
        skeleton,
        near_boxes,
        near_count.reshape(box_count, 1),
    )
    coupling = coupling.reshape(prior, all_columns, all_columns)
    return block, coupling, factor[:, :all_columns]


def solution(mesh):
    return jax.shard_map(
        shards,
        mesh=mesh,
        in_specs=(
            P(None, None, "col", "box"),
            P(None, "box"),
            P("box"),
            P("box", None, None),
            P("box", None),
            P("box", None),
            P("box"),
        ),
        out_specs=(P(None, "col", "box"), P(), P()),
        check_vma=False,
    )
```

```python
import functools
import math

import jax
import jax.numpy as jnp
from jax import lax
from jax.experimental import pallas as pl
from jax.experimental.pallas import tpu as pltpu
from jax.sharding import PartitionSpec as P

BOX_DEV = 4


WAVENUMBER = 6.0
SMOOTHING = 0.1
SHIFT_SCALE = 0.02
EPSILON = 1e-06
HIGHEST = lax.Precision.HIGHEST
GROUP = 8
QUARTER = math.pi / 2.0
UNIT = WAVENUMBER / QUARTER


def split(values):
    high = values.astype(jnp.bfloat16)
    return high, (values - high.astype(jnp.float32)).astype(jnp.bfloat16)


def pair_dot(values, kernel):
    rows = values.shape[0]
    value_high, value_low = split(values)
    kernel_high, kernel_low = split(kernel)
    both = jnp.dot(
        jnp.concatenate([value_high, value_low], axis=0),
        kernel_high,
        preferred_element_type=jnp.float32,
    )
    cross = jnp.dot(value_high, kernel_low, preferred_element_type=jnp.float32)
    return both[:rows] + both[rows:] + cross


def helmholtz_pair(sources, targets):
    spread = (SMOOTHING * UNIT) ** 2
    for axis_index in range(3):
        step = sources[:, axis_index : axis_index + 1] - targets[axis_index : axis_index + 1, :]
        spread = spread + step * step
    inverse = lax.rsqrt(spread)
    angle = spread * inverse
    factor = inverse * (UNIT / (4.0 * math.pi))
    turns = jnp.floor(angle + 0.5)
    quarter = turns.astype(jnp.int32)
    rest = angle - turns
    square = rest * rest
    sine = -1.9515295891e-4 * QUARTER**7 * square + 8.3321608736e-3 * QUARTER**5
    sine = (sine * square - 1.6666654611e-1 * QUARTER**3) * square + QUARTER
    sine = sine * rest
    cosine = 2.443315711809948e-5 * QUARTER**8 * square - 1.388731625493765e-3 * QUARTER**6
    cosine = (cosine * square + 4.166664568298827e-2 * QUARTER**4) * square - 0.5 * QUARTER**2
    cosine = cosine * square + 1.0
    odd = (quarter & 1) == 1
    sine, cosine = jnp.where(odd, cosine, sine), jnp.where(odd, sine, cosine)
    sine_factor = jnp.where((quarter & 2) == 2, -factor, factor)
    cosine_factor = jnp.where(((quarter + 1) & 2) == 2, -factor, factor)
    return cosine * cosine_factor, sine * sine_factor


def combine(product, columns, points):
    left, right = product[:, :points], product[:, points:]
    return jnp.concatenate(
        [left[:columns] - right[columns:], left[columns:] + right[:columns]], axis=0
    )


def peer_copy(axis, count, step, source, target, sems):
    peer = lax.rem(lax.axis_index(axis) + step, count)
    return pltpu.make_async_remote_copy(
        src_ref=source(peer),
        dst_ref=target,
        send_sem=sems[0].at[step],
        recv_sem=sems[1].at[step],
        device_id={axis: peer},
        device_id_type=pl.DeviceIdType.MESH,
    )


def start_all(axis, count, source, target, sems):
    def body(step, carry):
        peer_copy(axis, count, step, source, target, sems).start()
        return carry

    lax.fori_loop(1, count, body, 0)


def wait_all(axis, count, source, target, sems):
    def body(step, carry):
        peer_copy(axis, count, step, source, target, sems).wait()
        return carry

    lax.fori_loop(1, count, body, 0)


def exchange(axis, count, source, target, sems):
    start_all(axis, count, source, target, sems)
    wait_all(axis, count, source, target, sems)


def slot_sum(buffer, count):
    if count <= 16:
        total = buffer[0]
        for slot in range(1, count):
            total = total + buffer[slot]
        return total
    return lax.fori_loop(1, count, lambda slot, total: total + buffer[slot], buffer[0])


def greet(barrier, box_size, col_size):
    for axis, count in (("box", box_size), ("col", col_size)):

        def body(step, carry):
            peer = lax.rem(lax.axis_index(axis) + step, count)
            pl.semaphore_signal(
                barrier, inc=1, device_id={axis: peer}, device_id_type=pl.DeviceIdType.MESH
            )
            return carry

        lax.fori_loop(1, count, body, 0)


def nt_dot(left, right):
    return lax.dot_general(
        left,
        right,
        (((1,), (1,)), ((), ())),
        precision=HIGHEST,
        preferred_element_type=jnp.float32,
    )


def nn_dot(left, right):
    return jnp.dot(left, right, precision=HIGHEST, preferred_element_type=jnp.float32)


def factor_rows(matrix, size):
    row_index = lax.broadcasted_iota(jnp.int32, matrix.shape, 0)
    scale = jnp.ones_like(matrix)
    for first in range(0, size, GROUP):
        group = range(first, min(first + GROUP, size))
        columns = [jnp.broadcast_to(matrix[:, j : j + 1], matrix.shape) for j in group]
        rows = [matrix[j : j + 1, :] for j in group]
        update = jnp.zeros_like(matrix)
        for place, j in enumerate(group):
            pivot = columns[place][j : j + 1, :]
            inverse = 1.0 / pivot
            scaled = rows[place] * inverse
            scale = jnp.where(row_index == j, pivot, scale)
            for other in range(place + 1, len(rows)):
                entry = columns[place][first + other : first + other + 1, :]
                rows[other] = rows[other] - entry * scaled
                columns[other] = columns[other] - columns[place] * (entry * inverse)
            update = update + jnp.where(row_index > j, columns[place] * scaled, 0.0)
        matrix = matrix - update
    return matrix * lax.rsqrt(scale)


def step_kernel(
    box_size,
    col_size,
    basis_ref,
    offsets_ref,
    weights_ref,
    interp_ref,
    skeleton_ref,
    near_boxes_ref,
    near_count_ref,
    block_ref,
    coupling_ref,
    factor_ref,
    row_basis,
    row_applied,
    part,
    col_parts,
    box_parts,
    piece,
    whole,
    gram_mine,
    gram_cols,
    gram_sum,
    gram_boxes,
    normal,
    applied_ref,
    beside,
    column_pos,
    far_mine,
    far_all,
    near_times,
    far_times,
    near_total,
    far_total,
    *sems,
):
    sems = [(sems[2 * i], sems[2 * i + 1]) for i in range(11)]
    prior, _, columns, _ = basis_ref.shape
    all_columns, points = row_applied.shape[1:]
    col = lax.axis_index("col")
    box = lax.axis_index("box")
    share = all_columns // col_size
    row_total = points * box_size * col_size

    def rows_of(index, size):
        return pl.ds(pl.multiple_of(index * size, size), size)

    def basis_source(peer):
        return basis_ref.at[:, :, :, rows_of(peer, points)]

    def applied_source(peer):
        return applied_ref.at[:, :, rows_of(peer, points)]

    basis_target = row_basis.at[:, :, rows_of(col, columns), :]
    applied_target = row_applied.at[:, rows_of(col, columns), :]
    box_count, skel_count, box_points = interp_ref.shape
    rows = 2 * columns
    reach = box_count
    window = 2 * reach + 1
    first_box = box * box_count
    barrier = pltpu.get_barrier_semaphore()
    greet(barrier, box_size, col_size)

    def of_box(index):
        return slice(index * box_points, (index + 1) * box_points)

    local_points = box_count * box_points
    box_lane = lax.broadcasted_iota(jnp.int32, (1, local_points), 1) // box_points + first_box
    center_first = (box_lane // BOX_DEV).astype(jnp.float32)
    center_second = (box_lane % BOX_DEV).astype(jnp.float32)
    positions = jnp.concatenate(
        [
            offsets_ref[0:1, :] + center_first,
            offsets_ref[1:2, :] + center_second,
            offsets_ref[2:3, :],
            jnp.zeros((5, local_points), jnp.float32),
        ],
        axis=0,
    )
    positions = positions * UNIT
    current = basis_ref[prior - 1].reshape(rows, local_points)
    sources = current * weights_ref[...]
    beside[1, :rows, :] = sources
    beside[1, rows:, :] = positions
    pl.semaphore_wait(barrier, box_size + col_size - 2)
    after = lax.rem(box + 1, box_size)
    before = lax.rem(box + box_size - 1, box_size)
    side_copies = [
        pltpu.make_async_remote_copy(
            src_ref=beside.at[1],
            dst_ref=beside.at[slot],
            send_sem=sems[index][0].at[0],
            recv_sem=sems[index][1].at[0],
            device_id={"box": peer},
            device_id_type=pl.DeviceIdType.MESH,
        )
        for slot, peer, index in ((0, after, 8), (2, before, 9))
    ]
    for copy in side_copies:
        copy.start()
    flat_skel = box_count * skel_count
    interp = interp_ref[...].reshape(flat_skel, box_points)
    skel_box = lax.broadcasted_iota(jnp.int32, (1, flat_skel), 1) // skel_count
    skel_flat = jnp.concatenate([skeleton_ref[b : b + 1, :] for b in range(box_count)], axis=1)
    hot = (
        lax.broadcasted_iota(jnp.int32, (box_points, flat_skel), 0) == skel_flat
    ).astype(jnp.float32)
    charges = jnp.zeros((rows, flat_skel), jnp.float32)
    skel_pos = jnp.zeros((8, flat_skel), jnp.float32)
    stacked = nt_dot(
        jnp.concatenate([sources[:, of_box(b)] for b in range(box_count)], axis=0), interp
    )
    stacked_pos = nn_dot(
        jnp.concatenate([positions[:, of_box(b)] for b in range(box_count)], axis=0), hot
    )
    for b in range(box_count):
        charges = jnp.where(skel_box == b, stacked[b * rows : (b + 1) * rows], charges)
        skel_pos = jnp.where(skel_box == b, stacked_pos[b * 8 : (b + 1) * 8], skel_pos)
    far_mine[:rows, :] = charges
    far_mine[rows:, :] = skel_pos
    far_all[box] = far_mine[...]
    far_source = lambda peer: far_mine
    start_all("box", box_size, far_source, far_all.at[box], sems[10])
    start_all("col", col_size, basis_source, basis_target, sems[0])
    own_box = lax.broadcasted_iota(jnp.int32, (box_count, 1), 0) + first_box
    slots = lax.broadcasted_iota(jnp.int32, near_boxes_ref.shape, 1)
    count_index = lax.broadcasted_iota(jnp.int32, near_boxes_ref.shape, 0)
    counts = jnp.zeros(near_boxes_ref.shape, jnp.int32)
    for b in range(box_count):
        counts = jnp.where(count_index == b, near_count_ref[b], counts)
    distance = jnp.where(slots < counts, near_boxes_ref[...] - own_box, window)
    for o in range(window):
        times = jnp.sum((distance == o - reach).astype(jnp.float32), axis=1, keepdims=True)
        near_times[o] = jnp.broadcast_to(times, (box_count, box_points))
        listed = jnp.zeros((1, flat_skel), jnp.float32)
        for b in range(box_count):
            listed = jnp.where(skel_box == b, jnp.minimum(times[b : b + 1], 1.0), listed)
        far_times[o : o + 1, :] = listed
    near_total[...] = jnp.zeros_like(near_total)
    far_total[...] = jnp.zeros_like(far_total)
    for copy in side_copies:
        copy.wait()
    for slot in range(3):
        column_pos[slot * local_points : (slot + 1) * local_points, :] = beside[slot, rows:, :].T

    def near_step(o, carry):
        for b in range(box_count):
            extended = o + b
            lanes = rows_of(lax.rem(extended, box_count), box_points)
            values = beside[extended // box_count, :rows, lanes]
            values = values * near_times[o, b : b + 1, :]
            source_pos = column_pos[rows_of(extended, box_points), :]
            kernel = helmholtz_pair(source_pos, beside[1, rows:, of_box(b)])
            near_total[b] += pair_dot(values, jnp.concatenate(kernel, axis=1))
        return carry

    lax.fori_loop(0, window, near_step, 0)
    wait_all("box", box_size, far_source, far_all.at[box], sems[10])

    def far_step(slot, carry):
        source_pos = far_all[slot, rows:, :].T
        kernel_re, kernel_im = helmholtz_pair(source_pos, far_mine[rows:, :])
        source_box = lax.broadcasted_iota(jnp.int32, kernel_re.shape, 0) // skel_count
        offset = source_box + (slot * box_count - first_box + reach) - skel_box
        weight = jnp.ones_like(kernel_re)
        for o in range(window):
            weight = jnp.where(offset == o, 1.0 - far_times[o : o + 1, :], weight)
        kernel = jnp.concatenate([kernel_re * weight, kernel_im * weight], axis=1)
        far_total[...] += pair_dot(far_all[slot, :rows, :], kernel)
        return carry

    lax.fori_loop(0, box_size, far_step, 0)
    potentials = combine(far_total[...], columns, flat_skel)
    far_field = nn_dot(
        jnp.concatenate(
            [jnp.where(skel_box == b, potentials, 0.0) for b in range(box_count)], axis=0
        ),
        interp,
    )
    for b in range(box_count):
        field = combine(near_total[b], columns, box_points) + far_field[b * rows : (b + 1) * rows]
        field = 0.5 * current[:, of_box(b)] + field
        applied_ref[0, :, of_box(b)] = field[:columns]
        applied_ref[1, :, of_box(b)] = field[columns:]
    start_all("col", col_size, applied_source, applied_target, sems[1])
    row_basis[:, :, rows_of(col, columns), :] = basis_ref[:, :, :, rows_of(col, points)]
    row_applied[:, rows_of(col, columns), :] = applied_ref[:, :, rows_of(col, points)]
    wait_all("col", col_size, applied_source, applied_target, sems[1])
    wait_all("col", col_size, basis_source, basis_target, sems[0])
    flat_basis = jnp.concatenate(
        [
            row_basis[:, part_index].reshape(prior * all_columns, points)
            for part_index in range(2)
        ],
        axis=1,
    )
    flat_applied = jnp.concatenate([row_applied[0], row_applied[1]], axis=1)
    part[...] = nt_dot(flat_applied, flat_basis) * (1.0 / row_total)
    col_parts[col] = part[rows_of(col, share), :]
    exchange(
        "col", col_size, lambda peer: part.at[rows_of(peer, share), :], col_parts.at[col], sems[2]
    )
    piece[...] = slot_sum(col_parts, col_size)
    box_parts[box] = piece[...]
    exchange("box", box_size, lambda peer: piece, box_parts.at[box], sems[3])
    shared = slot_sum(box_parts, box_size)
    whole[rows_of(col, share), :] = shared
    piece[...] = shared
    exchange("col", col_size, lambda peer: piece, whole.at[rows_of(col, share), :], sems[4])
    coupling = whole[...]
    residual = flat_applied - nn_dot(coupling, flat_basis)
    blank = jnp.zeros_like(residual)
    gram_mine[...] = nt_dot(residual, jnp.concatenate([residual, blank], axis=0)) * (
        1.0 / row_total
    )
    gram_cols[col] = gram_mine[...]
    gram_source = lambda peer: gram_mine
    start_all("col", col_size, gram_source, gram_cols.at[col], sems[5])
    coupling_ref[...] = coupling.T
    wait_all("col", col_size, gram_source, gram_cols.at[col], sems[5])
    gram_sum[...] = slot_sum(gram_cols, col_size)
    gram_boxes[box] = gram_sum[...]
    exchange("box", box_size, lambda peer: gram_sum, gram_boxes.at[box], sems[6])
    gram = slot_sum(gram_boxes, box_size)
    row_index = lax.broadcasted_iota(jnp.int32, gram.shape, 0)
    lane_index = lax.broadcasted_iota(jnp.int32, gram.shape, 1)
    trace = jnp.sum(jnp.where(row_index == lane_index, gram, 0.0), keepdims=True)
    shift = trace * (SHIFT_SCALE / all_columns) + EPSILON
    matrix = gram + jnp.where(row_index == lane_index, shift, 0.0)
    matrix = matrix + jnp.where(row_index + all_columns == lane_index, 1.0, 0.0)
    reduced = factor_rows(matrix, all_columns)
    factor_ref[...] = jnp.where(lane_index >= row_index, reduced, 0.0)
    inverse = jnp.where(lane_index >= all_columns, reduced, 0.0)
    normalized = nn_dot(inverse, jnp.concatenate([blank, residual], axis=0))
    normal[0] = normalized[:, :points]
    normal[1] = normalized[:, points:]
    block_ref[:, :, rows_of(col, points)] = normal[:, rows_of(col, columns), :]
    exchange(
        "col",
        col_size,
        lambda peer: normal.at[:, rows_of(peer, columns), :],
        block_ref.at[:, :, rows_of(col, points)],
        sems[7],
    )


def shards(basis, offsets, weights, interp, skeleton, near_boxes, near_count):
    prior, parts, columns, local_points = basis.shape
    box_count, skel_count, box_points = interp.shape
    flat_skel = box_count * skel_count
    rows = parts * columns
    window = 2 * box_count + 1
    box_size, col_size = lax.axis_size("box"), lax.axis_size("col")
    all_columns, points = columns * col_size, local_points // col_size
    share = all_columns // col_size
    flat = prior * all_columns
    square = (all_columns, 2 * all_columns)
    shapes = [
        (prior, parts, all_columns, points),
        (parts, all_columns, points),
        (all_columns, flat),
        (col_size, share, flat),
        (box_size, share, flat),
        (share, flat),
        (all_columns, flat),
        square,
        (col_size,) + square,
        square,
        (box_size,) + square,
        (parts, all_columns, points),
        (parts, columns, local_points),
        (3, rows + 8, local_points),
        (3 * local_points, 8),
        (rows + 8, flat_skel),
        (box_size, rows + 8, flat_skel),
        (window, box_count, box_points),
        (window, flat_skel),
        (box_count, rows, 2 * box_points),
        (rows, 2 * flat_skel),
    ]
    sems = []
    for axis in ("col", "col", "col", "box", "col", "col", "box", "col", "", "", "box"):
        count = {"box": box_size, "col": col_size, "": 1}[axis]
        sems += [pltpu.SemaphoreType.DMA((count,))] * 2
    vmem = pl.BlockSpec(memory_space=pltpu.VMEM)
    block, coupling, factor = pl.pallas_call(
        functools.partial(step_kernel, box_size, col_size),
        out_shape=(
            jax.ShapeDtypeStruct((parts, columns, local_points), jnp.float32),
            jax.ShapeDtypeStruct((flat, all_columns), jnp.float32),
            jax.ShapeDtypeStruct(square, jnp.float32),
        ),
        in_specs=[vmem] * 6 + [pl.BlockSpec(memory_space=pltpu.SMEM)],
        out_specs=(vmem,) * 3,
        scratch_shapes=[pltpu.VMEM(shape, jnp.float32) for shape in shapes] + sems,
        compiler_params=pltpu.CompilerParams(
            collective_id=0, has_side_effects=True, vmem_limit_bytes=40 * 1024 * 1024
        ),
    )(
        basis,
        offsets,
        weights.reshape(1, local_points),
        interp,
        skeleton,
        near_boxes,
        near_count,
    )
    coupling = coupling.reshape(prior, all_columns, all_columns)
    return block, coupling, factor[:, :all_columns]


def solution(mesh):
    return jax.shard_map(
        shards,
        mesh=mesh,
        in_specs=(
            P(None, None, "col", "box"),
            P(None, "box"),
            P("box"),
            P("box", None, None),
            P("box", None),
            P("box", None),
            P("box"),
        ),
        out_specs=(P(None, "col", "box"), P(), P()),
        check_vma=False,
    )
```

```python
import functools
import math

import jax
import jax.numpy as jnp
from jax import lax
from jax.experimental import pallas as pl
from jax.experimental.pallas import tpu as pltpu
from jax.sharding import PartitionSpec as P

BOX_DEV = 4


WAVENUMBER = 6.0
SMOOTHING = 0.1
SHIFT_SCALE = 0.02
EPSILON = 1e-06
HIGHEST = lax.Precision.HIGHEST
GROUP = 8
QUARTER = math.pi / 2.0
UNIT = WAVENUMBER / QUARTER


def split(values):
    high = values.astype(jnp.bfloat16)
    return high, (values - high.astype(jnp.float32)).astype(jnp.bfloat16)


def pair_dot(values, kernel):
    rows = values.shape[0]
    value_high, value_low = split(values)
    kernel_high, kernel_low = split(kernel)
    both = jnp.dot(
        jnp.concatenate([value_high, value_low], axis=0),
        kernel_high,
        preferred_element_type=jnp.float32,
    )
    cross = jnp.dot(value_high, kernel_low, preferred_element_type=jnp.float32)
    return both[:rows] + both[rows:] + cross


def helmholtz_pair(sources, targets):
    spread = (SMOOTHING * UNIT) ** 2
    for axis_index in range(3):
        step = sources[:, axis_index : axis_index + 1] - targets[axis_index : axis_index + 1, :]
        spread = spread + step * step
    inverse = lax.rsqrt(spread)
    angle = spread * inverse
    factor = inverse * (UNIT / (4.0 * math.pi))
    turns = jnp.floor(angle + 0.5)
    quarter = turns.astype(jnp.int32)
    rest = angle - turns
    square = rest * rest
    sine = -1.9515295891e-4 * QUARTER**7 * square + 8.3321608736e-3 * QUARTER**5
    sine = (sine * square - 1.6666654611e-1 * QUARTER**3) * square + QUARTER
    sine = sine * rest
    cosine = 2.443315711809948e-5 * QUARTER**8 * square - 1.388731625493765e-3 * QUARTER**6
    cosine = (cosine * square + 4.166664568298827e-2 * QUARTER**4) * square - 0.5 * QUARTER**2
    cosine = cosine * square + 1.0
    odd = (quarter & 1) == 1
    sine, cosine = jnp.where(odd, cosine, sine), jnp.where(odd, sine, cosine)
    sine_factor = jnp.where((quarter & 2) == 2, -factor, factor)
    cosine_factor = jnp.where(((quarter + 1) & 2) == 2, -factor, factor)
    return cosine * cosine_factor, sine * sine_factor


def combine(product, columns, points):
    left, right = product[:, :points], product[:, points:]
    return jnp.concatenate(
        [left[:columns] - right[columns:], left[columns:] + right[:columns]], axis=0
    )


def peer_copy(axis, count, step, source, target, sems):
    peer = lax.rem(lax.axis_index(axis) + step, count)
    return pltpu.make_async_remote_copy(
        src_ref=source(peer),
        dst_ref=target,
        send_sem=sems[0].at[step],
        recv_sem=sems[1].at[step],
        device_id={axis: peer},
        device_id_type=pl.DeviceIdType.MESH,
    )


def start_all(axis, count, source, target, sems):
    def body(step, carry):
        peer_copy(axis, count, step, source, target, sems).start()
        return carry

    lax.fori_loop(1, count, body, 0)


def wait_all(axis, count, source, target, sems):
    def body(step, carry):
        peer_copy(axis, count, step, source, target, sems).wait()
        return carry

    lax.fori_loop(1, count, body, 0)


def exchange(axis, count, source, target, sems):
    start_all(axis, count, source, target, sems)
    wait_all(axis, count, source, target, sems)


def slot_sum(buffer, count):
    if count <= 16:
        total = buffer[0]
        for slot in range(1, count):
            total = total + buffer[slot]
        return total
    return lax.fori_loop(1, count, lambda slot, total: total + buffer[slot], buffer[0])


def greet(barrier, box_size, col_size):
    for axis, count in (("box", box_size), ("col", col_size)):

        def body(step, carry):
            peer = lax.rem(lax.axis_index(axis) + step, count)
            pl.semaphore_signal(
                barrier, inc=1, device_id={axis: peer}, device_id_type=pl.DeviceIdType.MESH
            )
            return carry

        lax.fori_loop(1, count, body, 0)


def nt_dot(left, right):
    return lax.dot_general(
        left,
        right,
        (((1,), (1,)), ((), ())),
        precision=HIGHEST,
        preferred_element_type=jnp.float32,
    )


def nn_dot(left, right):
    return jnp.dot(left, right, precision=HIGHEST, preferred_element_type=jnp.float32)


def factor_rows(matrix, size):
    row_index = lax.broadcasted_iota(jnp.int32, matrix.shape, 0)
    scale = jnp.ones_like(matrix)
    for first in range(0, size, GROUP):
        group = range(first, min(first + GROUP, size))
        columns = [jnp.broadcast_to(matrix[:, j : j + 1], matrix.shape) for j in group]
        rows = [matrix[j : j + 1, :] for j in group]
        update = jnp.zeros_like(matrix)
        for place, j in enumerate(group):
            pivot = columns[place][j : j + 1, :]
            inverse = 1.0 / pivot
            scaled = rows[place] * inverse
            scale = jnp.where(row_index == j, pivot, scale)
            for other in range(place + 1, len(rows)):
                entry = columns[place][first + other : first + other + 1, :]
                rows[other] = rows[other] - entry * scaled
                columns[other] = columns[other] - columns[place] * (entry * inverse)
            update = update + jnp.where(row_index > j, columns[place] * scaled, 0.0)
        matrix = matrix - update
    return matrix * lax.rsqrt(scale)


def step_kernel(
    box_size,
    col_size,
    basis_ref,
    offsets_ref,
    weights_ref,
    interp_ref,
    skeleton_ref,
    near_boxes_ref,
    near_count_ref,
    block_ref,
    coupling_ref,
    factor_ref,
    row_basis,
    row_applied,
    part,
    col_parts,
    box_parts,
    piece,
    whole,
    gram_mine,
    gram_cols,
    gram_sum,
    gram_boxes,
    normal,
    applied_ref,
    beside,
    column_pos,
    far_mine,
    far_all,
    near_times,
    far_times,
    near_total,
    far_total,
    *sems,
):
    sems = [(sems[2 * i], sems[2 * i + 1]) for i in range(11)]
    prior, _, columns, _ = basis_ref.shape
    all_columns, points = row_applied.shape[1:]
    col = lax.axis_index("col")
    box = lax.axis_index("box")
    share = all_columns // col_size
    row_total = points * box_size * col_size

    def rows_of(index, size):
        return pl.ds(pl.multiple_of(index * size, size), size)

    def basis_source(peer):
        return basis_ref.at[:, :, :, rows_of(peer, points)]

    def applied_source(peer):
        return applied_ref.at[:, :, rows_of(peer, points)]

    basis_target = row_basis.at[:, :, rows_of(col, columns), :]
    applied_target = row_applied.at[:, rows_of(col, columns), :]
    box_count, skel_count, box_points = interp_ref.shape
    rows = 2 * columns
    reach = box_count
    window = 2 * reach + 1
    first_box = box * box_count
    barrier = pltpu.get_barrier_semaphore()
    greet(barrier, box_size, col_size)

    def of_box(index):
        return slice(index * box_points, (index + 1) * box_points)

    local_points = box_count * box_points
    box_lane = lax.broadcasted_iota(jnp.int32, (1, local_points), 1) // box_points + first_box
    center_first = (box_lane // BOX_DEV).astype(jnp.float32)
    center_second = (box_lane % BOX_DEV).astype(jnp.float32)
    positions = jnp.concatenate(
        [
            offsets_ref[0:1, :] + center_first,
            offsets_ref[1:2, :] + center_second,
            offsets_ref[2:3, :],
            jnp.zeros((5, local_points), jnp.float32),
        ],
        axis=0,
    )
    positions = positions * UNIT
    current = basis_ref[prior - 1].reshape(rows, local_points)
    sources = current * weights_ref[...]
    beside[1, :rows, :] = sources
    beside[1, rows:, :] = positions
    pl.semaphore_wait(barrier, box_size + col_size - 2)
    after = lax.rem(box + 1, box_size)
    before = lax.rem(box + box_size - 1, box_size)
    side_copies = [
        pltpu.make_async_remote_copy(
            src_ref=beside.at[1],
            dst_ref=beside.at[slot],
            send_sem=sems[index][0].at[0],
            recv_sem=sems[index][1].at[0],
            device_id={"box": peer},
            device_id_type=pl.DeviceIdType.MESH,
        )
        for slot, peer, index in ((0, after, 8), (2, before, 9))
    ]
    for copy in side_copies:
        copy.start()
    flat_skel = box_count * skel_count
    interp = interp_ref[...].reshape(flat_skel, box_points)
    skel_box = lax.broadcasted_iota(jnp.int32, (1, flat_skel), 1) // skel_count
    skel_flat = jnp.concatenate([skeleton_ref[b : b + 1, :] for b in range(box_count)], axis=1)
    hot = (
        lax.broadcasted_iota(jnp.int32, (box_points, flat_skel), 0) == skel_flat
    ).astype(jnp.float32)
    charges = jnp.zeros((rows, flat_skel), jnp.float32)
    skel_pos = jnp.zeros((8, flat_skel), jnp.float32)
    stacked = nt_dot(
        jnp.concatenate([sources[:, of_box(b)] for b in range(box_count)], axis=0), interp
    )
    stacked_pos = nn_dot(
        jnp.concatenate([positions[:, of_box(b)] for b in range(box_count)], axis=0), hot
    )
    for b in range(box_count):
        charges = jnp.where(skel_box == b, stacked[b * rows : (b + 1) * rows], charges)
        skel_pos = jnp.where(skel_box == b, stacked_pos[b * 8 : (b + 1) * 8], skel_pos)
    far_mine[:rows, :] = charges
    far_mine[rows:, :] = skel_pos
    far_all[box] = far_mine[...]
    far_source = lambda peer: far_mine
    start_all("box", box_size, far_source, far_all.at[box], sems[10])
    start_all("col", col_size, basis_source, basis_target, sems[0])
    own_box = lax.broadcasted_iota(jnp.int32, (box_count, 1), 0) + first_box
    slots = lax.broadcasted_iota(jnp.int32, near_boxes_ref.shape, 1)
    count_index = lax.broadcasted_iota(jnp.int32, near_boxes_ref.shape, 0)
    counts = jnp.zeros(near_boxes_ref.shape, jnp.int32)
    for b in range(box_count):
        counts = jnp.where(count_index == b, near_count_ref[b], counts)
    distance = jnp.where(slots < counts, near_boxes_ref[...] - own_box, window)
    for o in range(window):
        times = jnp.sum((distance == o - reach).astype(jnp.float32), axis=1, keepdims=True)
        near_times[o] = jnp.broadcast_to(times, (box_count, box_points))
        listed = jnp.zeros((1, flat_skel), jnp.float32)
        for b in range(box_count):
            listed = jnp.where(skel_box == b, jnp.minimum(times[b : b + 1], 1.0), listed)
        far_times[o : o + 1, :] = listed
    near_total[...] = jnp.zeros_like(near_total)
    far_total[...] = jnp.zeros_like(far_total)
    for copy in side_copies:
        copy.wait()
    for slot in range(3):
        column_pos[slot * local_points : (slot + 1) * local_points, :] = beside[slot, rows:, :].T

    def near_step(o, carry):
        for b in range(box_count):
            extended = o + b
            lanes = rows_of(lax.rem(extended, box_count), box_points)
            values = beside[extended // box_count, :rows, lanes]
            values = values * near_times[o, b : b + 1, :]
            source_pos = column_pos[rows_of(extended, box_points), :]
            kernel = helmholtz_pair(source_pos, beside[1, rows:, of_box(b)])
            near_total[b] += pair_dot(values, jnp.concatenate(kernel, axis=1))
        return carry

    lax.fori_loop(0, window, near_step, 0)
    wait_all("box", box_size, far_source, far_all.at[box], sems[10])

    def far_step(slot, carry):
        source_pos = far_all[slot, rows:, :].T
        kernel_re, kernel_im = helmholtz_pair(source_pos, far_mine[rows:, :])
        source_box = lax.broadcasted_iota(jnp.int32, kernel_re.shape, 0) // skel_count
        offset = source_box + (slot * box_count - first_box + reach) - skel_box
        weight = jnp.ones_like(kernel_re)
        for o in range(window):
            weight = jnp.where(offset == o, 1.0 - far_times[o : o + 1, :], weight)
        kernel = jnp.concatenate([kernel_re * weight, kernel_im * weight], axis=1)
        far_total[...] += pair_dot(far_all[slot, :rows, :], kernel)
        return carry

    lax.fori_loop(0, box_size, far_step, 0)
    potentials = combine(far_total[...], columns, flat_skel)
    far_field = nn_dot(
        jnp.concatenate(
            [jnp.where(skel_box == b, potentials, 0.0) for b in range(box_count)], axis=0
        ),
        interp,
    )
    for b in range(box_count):
        field = combine(near_total[b], columns, box_points) + far_field[b * rows : (b + 1) * rows]
        field = 0.5 * current[:, of_box(b)] + field
        applied_ref[0, :, of_box(b)] = field[:columns]
        applied_ref[1, :, of_box(b)] = field[columns:]
    start_all("col", col_size, applied_source, applied_target, sems[1])
    row_basis[:, :, rows_of(col, columns), :] = basis_ref[:, :, :, rows_of(col, points)]
    row_applied[:, rows_of(col, columns), :] = applied_ref[:, :, rows_of(col, points)]
    wait_all("col", col_size, basis_source, basis_target, sems[0])
    flat_basis = jnp.concatenate(
        [
            row_basis[:, part_index].reshape(prior * all_columns, points)
            for part_index in range(2)
        ],
        axis=1,
    )
    wait_all("col", col_size, applied_source, applied_target, sems[1])
    flat_applied = jnp.concatenate([row_applied[0], row_applied[1]], axis=1)
    part[...] = nt_dot(flat_applied, flat_basis) * (1.0 / row_total)
    col_parts[col] = part[rows_of(col, share), :]
    exchange(
        "col", col_size, lambda peer: part.at[rows_of(peer, share), :], col_parts.at[col], sems[2]
    )
    piece[...] = slot_sum(col_parts, col_size)
    box_parts[box] = piece[...]
    exchange("box", box_size, lambda peer: piece, box_parts.at[box], sems[3])
    shared = slot_sum(box_parts, box_size)
    whole[rows_of(col, share), :] = shared
    piece[...] = shared
    exchange("col", col_size, lambda peer: piece, whole.at[rows_of(col, share), :], sems[4])
    coupling = whole[...]
    residual = flat_applied - nn_dot(coupling, flat_basis)
    blank = jnp.zeros_like(residual)
    gram_mine[...] = nt_dot(residual, jnp.concatenate([residual, blank], axis=0)) * (
        1.0 / row_total
    )
    gram_cols[col] = gram_mine[...]
    gram_source = lambda peer: gram_mine
    start_all("col", col_size, gram_source, gram_cols.at[col], sems[5])
    coupling_ref[...] = coupling.T
    wait_all("col", col_size, gram_source, gram_cols.at[col], sems[5])
    gram_sum[...] = slot_sum(gram_cols, col_size)
    gram_boxes[box] = gram_sum[...]
    exchange("box", box_size, lambda peer: gram_sum, gram_boxes.at[box], sems[6])
    gram = slot_sum(gram_boxes, box_size)
    row_index = lax.broadcasted_iota(jnp.int32, gram.shape, 0)
    lane_index = lax.broadcasted_iota(jnp.int32, gram.shape, 1)
    trace = jnp.sum(jnp.where(row_index == lane_index, gram, 0.0), keepdims=True)
    shift = trace * (SHIFT_SCALE / all_columns) + EPSILON
    matrix = gram + jnp.where(row_index == lane_index, shift, 0.0)
    matrix = matrix + jnp.where(row_index + all_columns == lane_index, 1.0, 0.0)
    reduced = factor_rows(matrix, all_columns)
    factor_ref[...] = jnp.where(lane_index >= row_index, reduced, 0.0)
    inverse = jnp.where(lane_index >= all_columns, reduced, 0.0)
    normalized = nn_dot(inverse, jnp.concatenate([blank, residual], axis=0))
    normal[0] = normalized[:, :points]
    normal[1] = normalized[:, points:]
    block_ref[:, :, rows_of(col, points)] = normal[:, rows_of(col, columns), :]
    exchange(
        "col",
        col_size,
        lambda peer: normal.at[:, rows_of(peer, columns), :],
        block_ref.at[:, :, rows_of(col, points)],
        sems[7],
    )


def shards(basis, offsets, weights, interp, skeleton, near_boxes, near_count):
    prior, parts, columns, local_points = basis.shape
    box_count, skel_count, box_points = interp.shape
    flat_skel = box_count * skel_count
    rows = parts * columns
    window = 2 * box_count + 1
    box_size, col_size = lax.axis_size("box"), lax.axis_size("col")
    all_columns, points = columns * col_size, local_points // col_size
    share = all_columns // col_size
    flat = prior * all_columns
    square = (all_columns, 2 * all_columns)
    shapes = [
        (prior, parts, all_columns, points),
        (parts, all_columns, points),
        (all_columns, flat),
        (col_size, share, flat),
        (box_size, share, flat),
        (share, flat),
        (all_columns, flat),
        square,
        (col_size,) + square,
        square,
        (box_size,) + square,
        (parts, all_columns, points),
        (parts, columns, local_points),
        (3, rows + 8, local_points),
        (3 * local_points, 8),
        (rows + 8, flat_skel),
        (box_size, rows + 8, flat_skel),
        (window, box_count, box_points),
        (window, flat_skel),
        (box_count, rows, 2 * box_points),
        (rows, 2 * flat_skel),
    ]
    sems = []
    for axis in ("col", "col", "col", "box", "col", "col", "box", "col", "", "", "box"):
        count = {"box": box_size, "col": col_size, "": 1}[axis]
        sems += [pltpu.SemaphoreType.DMA((count,))] * 2
    vmem = pl.BlockSpec(memory_space=pltpu.VMEM)
    block, coupling, factor = pl.pallas_call(
        functools.partial(step_kernel, box_size, col_size),
        out_shape=(
            jax.ShapeDtypeStruct((parts, columns, local_points), jnp.float32),
            jax.ShapeDtypeStruct((flat, all_columns), jnp.float32),
            jax.ShapeDtypeStruct(square, jnp.float32),
        ),
        in_specs=[vmem] * 6 + [pl.BlockSpec(memory_space=pltpu.SMEM)],
        out_specs=(vmem,) * 3,
        scratch_shapes=[pltpu.VMEM(shape, jnp.float32) for shape in shapes] + sems,
        compiler_params=pltpu.CompilerParams(
            collective_id=0, has_side_effects=True, vmem_limit_bytes=63 * 1024 * 1024
        ),
    )(
        basis,
        offsets,
        weights.reshape(1, local_points),
        interp,
        skeleton,
        near_boxes,
        near_count,
    )
    coupling = coupling.reshape(prior, all_columns, all_columns)
    return block, coupling, factor[:, :all_columns]


def solution(mesh):
    return jax.shard_map(
        shards,
        mesh=mesh,
        in_specs=(
            P(None, None, "col", "box"),
            P(None, "box"),
            P("box"),
            P("box", None, None),
            P("box", None),
            P("box", None),
            P("box"),
        ),
        out_specs=(P(None, "col", "box"), P(), P()),
        check_vma=False,
    )
```
